32 devices in a mesh: groups: 2 (over x), mp: 8 (over z, y), dp: 2 (over core).
Axes of the slice: x: 2, y: 2, z: 4, core: 2. Of those that a mesh axis runs over, the one named last changes fastest.
Arguments:
- acts: bfloat16 [512, 4096], P(('groups', 'dp')), parts along dimension 0, may hold values from -6 to 6
- out_grads: bfloat16 [512, 14336], P(('groups', 'dp'), 'mp'), parts along dimension 0, may hold values from -6 to 6
- basis_in: bfloat16 [4096, 4096], P(None, 'mp'), may hold values from -0.09375 to 0.09375
- basis_out: bfloat16 [14336, 14336], P('mp', 'dp'), may hold values from -0.046875 to 0.046875
- eigen: float32 [4096, 14336], P(None, ('dp', 'mp')), may hold values from 1 to 16
- lengths: int32 [16], P('groups'), parts along dimension 0, may hold values from 1 to 64, 256 in all
Outputs:
- preconditioned: bfloat16 [16, 32, 14336], P('groups', None, ('mp', 'dp')), parts along dimension 0
The draws below stay inside these ranges and needn't reach their ends.
There are 2 independent parts, one for each index of `groups`. The reference program is written for one: setup_inputs(seed, part) draws one part's arguments, and reference() takes and returns one part's arrays. A program takes and returns all parts, laid end to end along the dimension named above; an argument that names none is the same for every part. Nothing has to cross between parts.
Inputs may be any that keep to these rules, and one draw needn't show every extreme that they name: The sequences lie end to end in the 256 token rows; the lengths sum to 256 and the longest is exactly 64.
All inputs are finite; a program needn't handle non-finite values.
Results may differ from the reference program's by a relative error of at most 0.006.
Values may be sent and summed in bfloat16 or wider, within the bound.
A program may use at most 256 MiB of HBM per device.

```python
import math
import jax
import jax.numpy as jnp
import numpy as np
from jax import lax

D = 4096
FF = 14336
SEQS = 8
OUT_ROWS = 32
ROWS = 256
SEQ_MOST = 64


def level_of(own_key, extent, cuts, least, top_value):
    factor_of = 1.0
    for dim, blocks in cuts:
        steps = jax.random.uniform(jax.random.fold_in(jax.random.fold_in(own_key, 6), dim), (blocks,), jnp.float32, least / len(cuts), top_value / len(cuts))
        factor_of = factor_of * jnp.repeat(jnp.exp(steps), extent[dim] // blocks).reshape((-1,) + (1,) * (len(extent) - 1 - dim))
    return factor_of


def length_profile(count, total, reach, slope):
    portions = [(1 << 20) // math.isqrt(rank ** slope) + 1 for rank in range(2, count + 1)]
    rest, holding = total - reach - (count - 1), [1] * (count - 1)
    while rest > 0:
        movable = [i for i in range(count - 1) if holding[i] < reach]
        pool, remaining = sum([portions[i] for i in movable]), rest
        for i in movable:
            extra = min(reach - holding[i], max(1, remaining * portions[i] // pool), rest)
            holding[i] = holding[i] + extra
            rest = rest - extra
    return np.array([reach] + holding)


def ragged(rng, amount, total, most, slope):
    if amount == 2:
        one = jax.random.randint(rng, (), max(1, total - most), min(most, total - 1) + 1)
        return jnp.stack([one, total - one])
    tallies = jnp.asarray(length_profile(amount, total, most, slope), jnp.int32)
    couples = (amount - 1) // 2
    source_of, taker = tallies[1:1 + 2 * couples:2], tallies[2:2 + 2 * couples:2]
    margin = jnp.minimum(source_of - 1, most - taker)
    moved = jax.random.randint(jax.random.fold_in(rng, 1), (couples,), 0, 1 << 20) % (margin + 1)
    tallies = tallies.at[1:1 + 2 * couples:2].set(source_of - moved).at[2:2 + 2 * couples:2].set(taker + moved)
    return tallies[jax.random.permutation(jax.random.fold_in(rng, 2), amount)]


def scatter_about(stream_key, dims, width, bound, pieces=(), kind=jnp.bfloat16):
    drawn = width * jax.random.normal(stream_key, dims, jnp.float32)
    if pieces:
        drawn = drawn * level_of(stream_key, dims, pieces, -0.22, 0.18)
    return jnp.clip(drawn, -bound, bound).astype(kind)


def setup_inputs(seed: int = 0, part: int = 0) -> dict:
    arg_keys = jax.random.split(jax.random.key(seed), 7)
    part_keys = jax.random.split(jax.random.fold_in(arg_keys[6], part), 7)
    acts = scatter_about(part_keys[0], (ROWS, D), 1.0, 6.0, ((0, 2),))
    out_grads = scatter_about(part_keys[1], (ROWS, FF), 1.0, 6.0, ((0, 2), (1, 8)))
    basis_in = scatter_about(arg_keys[2], (D, D), D ** -0.5, 0.09375, ((1, 8),))
    basis_out = scatter_about(arg_keys[3], (FF, FF), FF ** -0.5, 0.046875, ((0, 8), (1, 2)))
    eigen = jnp.clip(jnp.exp(math.log(16.0) - 2.7725887 * jax.random.uniform(arg_keys[4], (D, FF), jnp.float32) ** level_of(arg_keys[4], (D, FF), ((1, 16),), -0.2, 0.2)), 1.0, 16.0)
    lengths = ragged(part_keys[5], SEQS, ROWS, SEQ_MOST, 1).astype(jnp.int32)
    return {"acts": acts, "out_grads": out_grads, "basis_in": basis_in, "basis_out": basis_out, "eigen": eigen, "lengths": lengths}


def reference(acts, out_grads, basis_in, basis_out, eigen, lengths):
    rot_in = jnp.dot(acts, basis_in, preferred_element_type=jnp.float32).astype(jnp.bfloat16)
    rot_out = jnp.dot(out_grads, basis_out, preferred_element_type=jnp.float32).astype(jnp.bfloat16)
    seq_ends = jnp.cumsum(lengths).astype(jnp.int32)
    seq_starts = (seq_ends - lengths).astype(jnp.int32)
    position = jnp.arange(ROWS, dtype=jnp.int32)
    member = ((position[None, :] >= seq_starts[:, None]) & (position[None, :] < seq_ends[:, None])).astype(jnp.bfloat16)
    rows_back = basis_in[:OUT_ROWS]

    def single(weights):
        masked = rot_out * weights[:, None]
        unscaled = jnp.dot(rot_in.T, masked, preferred_element_type=jnp.float32)
        scaled = (unscaled / eigen).astype(jnp.bfloat16)
        back_rot = jnp.dot(rows_back, scaled, preferred_element_type=jnp.float32).astype(jnp.bfloat16)
        return jnp.dot(back_rot, basis_out.T, preferred_element_type=jnp.float32).astype(jnp.bfloat16)

    return lax.map(single, member)
```

```python
import functools

import jax
import jax.numpy as jnp
from jax import lax
from jax.experimental import pallas as pl
from jax.experimental.pallas import tpu as pltpu
from jax.sharding import PartitionSpec as P

OUT_ROWS = 32
BF16 = jnp.bfloat16
F32 = jnp.float32


def fold_kernel(member, rot_in_t, rot_out_t, eigen, rows_back, out, masked, total):
    seqs = total.shape[0]
    step = pl.program_id(0)

    @pl.when(step == 0)
    def _():
        for s in range(seqs):
            masked[s] = rot_out_t[...] * member[s : s + 1, :]
        total[...] = jnp.zeros_like(total)

    inverse = 1.0 / eigen[...]
    feats = rot_in_t[...]
    rows = rows_back[...]
    for s in range(seqs):
        unscaled = lax.dot_general(
            feats, masked[s], (((1,), (1,)), ((), ())), preferred_element_type=F32
        )
        scaled = (unscaled * inverse).astype(BF16)
        total[s] += jnp.dot(rows, scaled, preferred_element_type=F32)

    @pl.when(step == pl.num_programs(0) - 1)
    def _():
        out[...] = total[...].astype(out.dtype)


def fold(member, rot_in_t, rot_out_t, eigen, rows_back, block=256):
    seqs, tokens = member.shape
    feats, cols = eigen.shape
    rows = rows_back.shape[0]
    return pl.pallas_call(
        fold_kernel,
        grid=(feats // block,),
        in_specs=[
            pl.BlockSpec((seqs, tokens), lambda k: (0, 0)),
            pl.BlockSpec((block, tokens), lambda k: (k, 0)),
            pl.BlockSpec((cols, tokens), lambda k: (0, 0)),
            pl.BlockSpec((block, cols), lambda k: (k, 0)),
            pl.BlockSpec((rows, block), lambda k: (0, k)),
        ],
        out_specs=pl.BlockSpec((seqs, rows, cols), lambda k: (0, 0, 0)),
        out_shape=jax.ShapeDtypeStruct((seqs, rows, cols), BF16),
        scratch_shapes=[
            pltpu.VMEM((seqs, cols, tokens), BF16),
            pltpu.VMEM((seqs, rows, cols), F32),
        ],
        compiler_params=pltpu.CompilerParams(vmem_limit_bytes=40 * 2**20),
        cost_estimate=pl.CostEstimate(
            flops=2 * seqs * feats * cols * (tokens + 256),
            bytes_accessed=feats * cols * 4,
            transcendentals=0,
        ),
    )(member, rot_in_t, rot_out_t, eigen, rows_back)


def on_device(acts, out_grads, basis_in, basis_out, eigen, lengths):
    rot_local = jnp.dot(acts, basis_in, preferred_element_type=F32).astype(BF16)
    rot_in = lax.all_gather(rot_local, "dp", axis=0, tiled=True)
    grads_all = lax.all_gather(out_grads, "dp", axis=0, tiled=True)
    tokens = rot_in.shape[0]
    seq_ends = jnp.cumsum(lengths)
    seq_starts = seq_ends - lengths
    position = jnp.arange(tokens, dtype=jnp.int32)
    member = (
        (position[None, :] >= seq_starts[:, None]) & (position[None, :] < seq_ends[:, None])
    ).astype(BF16)

    partial = lax.dot_general(
        basis_out, grads_all, (((0,), (1,)), ((), ())), preferred_element_type=F32
    ).astype(BF16)
    rot_out_t = lax.psum_scatter(partial, "mp", scatter_dimension=0, tiled=True)

    rot_in_t = lax.all_gather(rot_in.T, "mp", axis=0, tiled=True)
    rows_back = lax.all_gather(basis_in[:OUT_ROWS], "mp", axis=1, tiled=True)
    back_rot = fold(member, rot_in_t, rot_out_t, eigen, rows_back)
    partial_out = jnp.einsum(
        "sok,fk->sof",
        lax.all_gather(back_rot, "mp", axis=2, tiled=True),
        basis_out,
        preferred_element_type=F32,
    )
    return lax.psum_scatter(partial_out, "dp", scatter_dimension=2, tiled=True).astype(BF16)


def solution(mesh):
    placed = (
        P(("groups", "dp"), None),
        P(("groups", "dp"), "mp"),
        P(None, "mp"),
        P("mp", "dp"),
        P(None, ("dp", "mp")),
        P("groups"),
    )
    return jax.shard_map(
        on_device,
        mesh=mesh,
        in_specs=placed,
        out_specs=P("groups", None, ("mp", "dp")),
        check_vma=False,
    )
```

```python
import functools

import jax
import jax.numpy as jnp
from jax import lax
from jax.experimental import pallas as pl
from jax.experimental.pallas import tpu as pltpu
from jax.sharding import PartitionSpec as P

OUT_ROWS = 32
BF16 = jnp.bfloat16
F32 = jnp.float32
MESH = pl.DeviceIdType.MESH


def fold_kernel(member, rot_in_t, rot_out_t, eigen, rows_back, out, masked, total):
    seqs = total.shape[0]
    step = pl.program_id(0)

    @pl.when(step == 0)
    def _():
        for s in range(seqs):
            masked[s] = rot_out_t[...] * member[s : s + 1, :]
        total[...] = jnp.zeros_like(total)

    inverse = 1.0 / eigen[...]
    feats = rot_in_t[...]
    rows = rows_back[...]
    for s in range(seqs):
        unscaled = lax.dot_general(
            feats, masked[s], (((1,), (1,)), ((), ())), preferred_element_type=F32
        )
        scaled = (unscaled * inverse).astype(BF16)
        total[s] += jnp.dot(rows, scaled, preferred_element_type=F32)

    @pl.when(step == pl.num_programs(0) - 1)
    def _():
        out[...] = total[...].astype(out.dtype)


def fold(member, rot_in_t, rot_out_t, eigen, rows_back, block=256):
    seqs, tokens = member.shape
    feats, cols = eigen.shape
    rows = rows_back.shape[0]
    return pl.pallas_call(
        fold_kernel,
        grid=(feats // block,),
        in_specs=[
            pl.BlockSpec((seqs, tokens), lambda k: (0, 0)),
            pl.BlockSpec((block, tokens), lambda k: (k, 0)),
            pl.BlockSpec((cols, tokens), lambda k: (0, 0)),
            pl.BlockSpec((block, cols), lambda k: (k, 0)),
            pl.BlockSpec((rows, block), lambda k: (0, k)),
        ],
        out_specs=pl.BlockSpec((seqs, rows, cols), lambda k: (0, 0, 0)),
        out_shape=jax.ShapeDtypeStruct((seqs, rows, cols), BF16),
        scratch_shapes=[
            pltpu.VMEM((seqs, cols, tokens), BF16),
            pltpu.VMEM((seqs, rows, cols), F32),
        ],
        compiler_params=pltpu.CompilerParams(vmem_limit_bytes=40 * 2**20),
        cost_estimate=pl.CostEstimate(
            flops=2 * seqs * feats * cols * (tokens + 256),
            bytes_accessed=feats * cols * 4,
            transcendentals=0,
        ),
    )(member, rot_in_t, rot_out_t, eigen, rows_back)


def scatter_kernel(
    n, grads, panel, out, blocks, own, ysend, yrecv, zsend, zrecv,
    block_sem, ys_sem, yr_sem, zs_sem, zr_sem,
):
    cols = out.shape[1]
    half = n // 2
    me = lax.axis_index("mp")
    y, z = lax.rem(me, 2), lax.div(me, 2)
    partner, above, below = me + 1 - 2 * y, me + 2, me - 2
    has_above, has_below = z < half - 1, z > 0

    def row(i):
        rising = jnp.where(i < half - 1 - z, half - 1 - i, i - (half - 1 - z))
        falling = jnp.where(i < z, i, half - 1 - (i - z))
        return jnp.where(2 * z < half, rising, falling)

    def block_copy(i, j):
        lane = jnp.where(j == 0, 1 - y, y)
        start = pl.multiple_of((row(i) * 2 + lane) * cols, 128)
        return pltpu.make_async_copy(
            panel.at[:, pl.ds(start, cols)], blocks.at[2 * i + j], block_sem.at[2 * i + j]
        )

    def y_copy(i):
        return pltpu.make_async_remote_copy(
            src_ref=ysend.at[i], dst_ref=yrecv.at[i], send_sem=ys_sem.at[i],
            recv_sem=yr_sem.at[i], device_id={"mp": partner}, device_id_type=MESH,
        )

    def z_copy(i, way, target):
        slot = row(i)
        return pltpu.make_async_remote_copy(
            src_ref=zsend.at[i], dst_ref=zrecv.at[way, slot], send_sem=zs_sem.at[i],
            recv_sem=zr_sem.at[way, slot], device_id={"mp": target}, device_id_type=MESH,
        )

    for i in range(half):
        for j in range(2):
            block_copy(i, j).start()
    greet(partner, above, below, has_above, has_below)

    def products(i, carry):
        block_copy(i, 0).wait()
        ysend[i] = jnp.dot(
            grads[...], blocks[2 * i], preferred_element_type=F32
        ).astype(BF16)
        y_copy(i).start()
        block_copy(i, 1).wait()
        own[i] = jnp.dot(grads[...], blocks[2 * i + 1], preferred_element_type=F32)
        return carry

    lax.fori_loop(0, half, products, 0)

    for i in range(half):
        y_copy(i).wait_recv()
        own[i] += yrecv[i].astype(F32)
        slot = row(i)
        upward, downward = slot > z, slot < z
        if i == half - 1:
            upward = downward = True

        @pl.when(jnp.logical_and(upward, has_below))
        def _():
            z_copy(i, 0, above).wait_recv()
            own[i] += zrecv[0, slot].astype(F32)

        @pl.when(jnp.logical_and(downward, has_above))
        def _():
            z_copy(i, 1, below).wait_recv()
            own[i] += zrecv[1, slot].astype(F32)

        if i < half - 1:
            zsend[i] = own[i].astype(BF16)

            @pl.when(upward)
            def _():
                z_copy(i, 0, above).start()

            @pl.when(downward)
            def _():
                z_copy(i, 1, below).start()
        else:
            out[...] = own[i].astype(BF16)

    for i in range(half):
        y_copy(i).wait_send()
        if i < half - 1:
            z_copy(i, 0, above).wait_send()


def greet(partner, above, below, has_above, has_below, core=None):
    barrier = pltpu.get_barrier_semaphore()
    pl.semaphore_signal(barrier, inc=1, device_id={"mp": partner}, device_id_type=MESH)
    if core is not None:
        pl.semaphore_signal(barrier, inc=1, device_id={"dp": core}, device_id_type=MESH)

    @pl.when(has_above)
    def _():
        pl.semaphore_signal(barrier, inc=1, device_id={"mp": above}, device_id_type=MESH)

    @pl.when(has_below)
    def _():
        pl.semaphore_signal(barrier, inc=1, device_id={"mp": below}, device_id_type=MESH)

    fixed = 1 if core is None else 2
    pl.semaphore_wait(
        barrier, fixed + has_above.astype(jnp.int32) + has_below.astype(jnp.int32)
    )


def scatter_sum(n, grads, panel):
    tokens, depth = grads.shape
    cols = panel.shape[1] // n
    half = n // 2
    return pl.pallas_call(
        functools.partial(scatter_kernel, n),
        in_specs=[
            pl.BlockSpec(memory_space=pltpu.VMEM),
            pl.BlockSpec(memory_space=pl.ANY),
        ],
        out_specs=pl.BlockSpec(memory_space=pltpu.VMEM),
        out_shape=jax.ShapeDtypeStruct((tokens, cols), BF16),
        scratch_shapes=[
            pltpu.VMEM((n, depth, cols), BF16),
            pltpu.VMEM((half, tokens, cols), F32),
            pltpu.VMEM((half, tokens, cols), BF16),
            pltpu.VMEM((half, tokens, cols), BF16),
            pltpu.VMEM((half, tokens, cols), BF16),
            pltpu.VMEM((2, half, tokens, cols), BF16),
            pltpu.SemaphoreType.DMA((n,)),
            pltpu.SemaphoreType.DMA((half,)),
            pltpu.SemaphoreType.DMA((half,)),
            pltpu.SemaphoreType.DMA((half,)),
            pltpu.SemaphoreType.DMA((2, half)),
        ],
        compiler_params=pltpu.CompilerParams(
            collective_id=0, has_side_effects=True, vmem_limit_bytes=48 * 2**20
        ),
        cost_estimate=pl.CostEstimate(
            flops=2 * tokens * depth * cols * n,
            bytes_accessed=panel.size * 2,
            transcendentals=0,
        ),
    )(grads, panel)


def on_device(acts, out_grads, basis_in, basis_out, eigen, lengths):
    rot_local = jnp.dot(acts, basis_in, preferred_element_type=F32).astype(BF16)
    grads_all = lax.all_gather(out_grads, "dp", axis=0, tiled=True)
    tokens = grads_all.shape[0]
    seq_ends = jnp.cumsum(lengths)
    seq_starts = seq_ends - lengths
    position = jnp.arange(tokens, dtype=jnp.int32)
    member = (
        (position[None, :] >= seq_starts[:, None]) & (position[None, :] < seq_ends[:, None])
    ).astype(BF16)

    ranks = lax.axis_size("mp")
    if ranks % 2 == 0 and eigen.shape[1] % 128 == 0:
        rot_out_t = scatter_sum(ranks, grads_all, basis_out).T
    else:
        partial = lax.dot_general(
            basis_out, grads_all, (((0,), (1,)), ((), ())), preferred_element_type=F32
        ).astype(BF16)
        rot_out_t = lax.psum_scatter(partial, "mp", scatter_dimension=0, tiled=True)

    shared = jnp.concatenate([rot_local, basis_in[:OUT_ROWS]], axis=0)
    shared = lax.all_gather(shared, "mp", axis=1, tiled=True)
    rows_back = shared[rot_local.shape[0] :]
    rot_in_t = lax.all_gather(shared[: rot_local.shape[0]], "dp", axis=0, tiled=True).T
    back_rot = fold(member, rot_in_t, rot_out_t, eigen, rows_back)
    partial_out = jnp.einsum(
        "sok,fk->sof",
        lax.all_gather(back_rot, "mp", axis=2, tiled=True),
        basis_out,
        preferred_element_type=F32,
    )
    return lax.psum_scatter(partial_out, "dp", scatter_dimension=2, tiled=True).astype(BF16)


def solution(mesh):
    placed = (
        P(("groups", "dp"), None),
        P(("groups", "dp"), "mp"),
        P(None, "mp"),
        P("mp", "dp"),
        P(None, ("dp", "mp")),
        P("groups"),
    )
    return jax.shard_map(
        on_device,
        mesh=mesh,
        in_specs=placed,
        out_specs=P("groups", None, ("mp", "dp")),
        check_vma=False,
    )
```

```python
import functools

import jax
import jax.numpy as jnp
from jax import lax
from jax.experimental import pallas as pl
from jax.experimental.pallas import tpu as pltpu
from jax.sharding import PartitionSpec as P

OUT_ROWS = 32
BF16 = jnp.bfloat16
F32 = jnp.float32
MESH = pl.DeviceIdType.MESH


def scatter_kernel(
    n, grads, panel, out, blocks, own, ysend, yrecv, zsend, zrecv,
    block_sem, ys_sem, yr_sem, zs_sem, zr_sem,
):
    cols = out.shape[1]
    half = n // 2
    me = lax.axis_index("mp")
    y, z = lax.rem(me, 2), lax.div(me, 2)
    partner, above, below = me + 1 - 2 * y, me + 2, me - 2
    has_above, has_below = z < half - 1, z > 0

    def row(i):
        rising = jnp.where(i < half - 1 - z, half - 1 - i, i - (half - 1 - z))
        falling = jnp.where(i < z, i, half - 1 - (i - z))
        return jnp.where(2 * z < half, rising, falling)

    def block_copy(i, j):
        lane = jnp.where(j == 0, 1 - y, y)
        start = pl.multiple_of((row(i) * 2 + lane) * cols, 128)
        return pltpu.make_async_copy(
            panel.at[:, pl.ds(start, cols)], blocks.at[2 * i + j], block_sem.at[2 * i + j]
        )

    def y_copy(i):
        return pltpu.make_async_remote_copy(
            src_ref=ysend.at[i], dst_ref=yrecv.at[i], send_sem=ys_sem.at[i],
            recv_sem=yr_sem.at[i], device_id={"mp": partner}, device_id_type=MESH,
        )

    def z_copy(i, way, target):
        slot = row(i)
        return pltpu.make_async_remote_copy(
            src_ref=zsend.at[i], dst_ref=zrecv.at[way, slot], send_sem=zs_sem.at[i],
            recv_sem=zr_sem.at[way, slot], device_id={"mp": target}, device_id_type=MESH,
        )

    for i in range(half):
        for j in range(2):
            block_copy(i, j).start()
    greet(partner, above, below, has_above, has_below)

    def products(i, carry):
        block_copy(i, 0).wait()
        ysend[i] = jnp.dot(
            grads[...], blocks[2 * i], preferred_element_type=F32
        ).astype(BF16)
        y_copy(i).start()
        block_copy(i, 1).wait()
        own[i] = jnp.dot(grads[...], blocks[2 * i + 1], preferred_element_type=F32)
        return carry

    lax.fori_loop(0, half, products, 0)

    for i in range(half):
        y_copy(i).wait_recv()
        own[i] += yrecv[i].astype(F32)
        slot = row(i)
        upward, downward = slot > z, slot < z
        if i == half - 1:
            upward = downward = True

        @pl.when(jnp.logical_and(upward, has_below))
        def _():
            z_copy(i, 0, above).wait_recv()
            own[i] += zrecv[0, slot].astype(F32)

        @pl.when(jnp.logical_and(downward, has_above))
        def _():
            z_copy(i, 1, below).wait_recv()
            own[i] += zrecv[1, slot].astype(F32)

        if i < half - 1:
            zsend[i] = own[i].astype(BF16)

            @pl.when(upward)
            def _():
                z_copy(i, 0, above).start()

            @pl.when(downward)
            def _():
                z_copy(i, 1, below).start()
        else:
            out[...] = own[i].astype(BF16)

    for i in range(half):
        y_copy(i).wait_send()
        if i < half - 1:
            z_copy(i, 0, above).wait_send()


def greet(partner, above, below, has_above, has_below, core=None):
    barrier = pltpu.get_barrier_semaphore()
    pl.semaphore_signal(barrier, inc=1, device_id={"mp": partner}, device_id_type=MESH)
    if core is not None:
        pl.semaphore_signal(barrier, inc=1, device_id={"dp": core}, device_id_type=MESH)

    @pl.when(has_above)
    def _():
        pl.semaphore_signal(barrier, inc=1, device_id={"mp": above}, device_id_type=MESH)

    @pl.when(has_below)
    def _():
        pl.semaphore_signal(barrier, inc=1, device_id={"mp": below}, device_id_type=MESH)

    fixed = 1 if core is None else 2
    pl.semaphore_wait(
        barrier, fixed + has_above.astype(jnp.int32) + has_below.astype(jnp.int32)
    )


def scatter_sum(n, grads, panel):
    tokens, depth = grads.shape
    cols = panel.shape[1] // n
    half = n // 2
    return pl.pallas_call(
        functools.partial(scatter_kernel, n),
        in_specs=[
            pl.BlockSpec(memory_space=pltpu.VMEM),
            pl.BlockSpec(memory_space=pl.ANY),
        ],
        out_specs=pl.BlockSpec(memory_space=pltpu.VMEM),
        out_shape=jax.ShapeDtypeStruct((tokens, cols), BF16),
        scratch_shapes=[
            pltpu.VMEM((n, depth, cols), BF16),
            pltpu.VMEM((half, tokens, cols), F32),
            pltpu.VMEM((half, tokens, cols), BF16),
            pltpu.VMEM((half, tokens, cols), BF16),
            pltpu.VMEM((half, tokens, cols), BF16),
            pltpu.VMEM((2, half, tokens, cols), BF16),
            pltpu.SemaphoreType.DMA((n,)),
            pltpu.SemaphoreType.DMA((half,)),
            pltpu.SemaphoreType.DMA((half,)),
            pltpu.SemaphoreType.DMA((half,)),
            pltpu.SemaphoreType.DMA((2, half)),
        ],
        compiler_params=pltpu.CompilerParams(
            collective_id=0, has_side_effects=True, vmem_limit_bytes=48 * 2**20
        ),
        cost_estimate=pl.CostEstimate(
            flops=2 * tokens * depth * cols * n,
            bytes_accessed=panel.size * 2,
            transcendentals=0,
        ),
    )(grads, panel)


def spans(cols, width=256):
    return [(start, min(width, cols - start)) for start in range(0, cols, width)]


def fold_kernel(
    n, block, member, rot_in_t, rot_out, eigen, rows_back, panel, out,
    eig, blocks, masked, total, acc, swap, *rest,
):
    parts = spans(out.shape[1])
    chunks = len(parts)
    held = rest[:chunks]
    eig_sem, block_sem, send_sem, recv_sem, swap_send, swap_recv = rest[chunks:]
    feats, cols = eigen.shape
    seqs, rows = member.shape[1], rows_back.shape[0]
    half = n // 2
    me, core = lax.axis_index("mp"), lax.axis_index("dp")
    y, z = lax.rem(me, 2), lax.div(me, 2)
    partner, above, below = me + 1 - 2 * y, me + 2, me - 2
    has_above, has_below = z < half - 1, z > 0

    def eig_copy(c):
        start, width = parts[c]
        span = pl.ds(start, width)
        return pltpu.make_async_copy(eigen.at[:, span], eig.at[:, span], eig_sem.at[c])

    def block_copy(d):
        start = pl.multiple_of(d * cols, 128)
        return pltpu.make_async_copy(
            panel.at[:, pl.ds(start, cols)], blocks.at[d], block_sem.at[d]
        )

    def pass_on(c, place, kind):
        slot = place * 2 + y
        return pltpu.make_async_remote_copy(
            src_ref=held[c].at[slot], dst_ref=held[c].at[slot],
            send_sem=send_sem.at[c, place, kind], recv_sem=recv_sem.at[c, slot],
            device_id={"mp": (partner, above, below)[kind]}, device_id_type=MESH,
        )

    def arrived(c, slot):
        pltpu.make_async_remote_copy(
            src_ref=held[c].at[slot], dst_ref=held[c].at[slot],
            send_sem=send_sem.at[c, 0, 0], recv_sem=recv_sem.at[c, slot],
            device_id={"mp": partner}, device_id_type=MESH,
        ).wait_recv()

    def send_own(c):
        @pl.when(has_above)
        def _():
            pass_on(c, z, 1).start()

        @pl.when(has_below)
        def _():
            pass_on(c, z, 2).start()

        pass_on(c, z, 0).start()

    def hop(c, h):
        @pl.when(z - h >= 0)
        def _():
            arrived(c, (z - h) * 2 + y)

            @pl.when(has_above)
            def _():
                pass_on(c, z - h, 1).start()

            pass_on(c, z - h, 0).start()

        @pl.when(z + h <= half - 1)
        def _():
            arrived(c, (z + h) * 2 + y)

            @pl.when(has_below)
            def _():
                pass_on(c, z + h, 2).start()

            pass_on(c, z + h, 0).start()

    def events(unit):
        for c in range(chunks):
            h = unit - 2 * (c + 1)
            if h == 0:
                send_own(c)
            elif 0 < h < half:
                hop(c, h)

    def fold_part(c, low, high):
        start, width = parts[c]

        def body(k, carry):
            at = pl.ds(pl.multiple_of(k * block, block), block)
            inverse = 1.0 / eig[at, start : start + width]
            unscaled = jnp.dot(
                rot_in_t[at, :], masked[:, : seqs * width], preferred_element_type=F32
            )
            scaled = (unscaled * jnp.concatenate([inverse] * seqs, axis=1)).astype(BF16)
            total[:, : seqs * width] += jnp.dot(
                rows_back[:, at], scaled, preferred_element_type=F32
            )
            return carry

        lax.fori_loop(low, high, body, 0)

    def project(c, low, high, part, wait):
        start, width = parts[c]
        at = pl.ds(pl.multiple_of(part * cols, 128), cols)

        def body(d, carry):
            if wait:

                @pl.when(lax.rem(d, 2) != y)
                def _():
                    arrived(c, d)

            acc[part] += lax.dot_general(
                held[c][d], blocks[d, at, start : start + width],
                (((1,), (1,)), ((), ())), preferred_element_type=F32,
            )
            return carry

        lax.fori_loop(low, high, body, 0)

    for c in range(chunks):
        eig_copy(c).start()
    for d in range(n):
        block_copy(d).start()
    greet(partner, above, below, has_above, has_below, 1 - core)

    steps = feats // block
    for c, (start, width) in enumerate(parts):
        for s in range(seqs):
            masked[:, s * width : (s + 1) * width] = (
                rot_out[:, start : start + width] * member[:, s : s + 1]
            )
        total[...] = jnp.zeros_like(total)
        eig_copy(c).wait()
        fold_part(c, 0, steps // 2)
        events(2 * c + 1)
        fold_part(c, steps // 2, steps)
        for s in range(seqs):
            held[c][me, s * rows : (s + 1) * rows, :] = total[
                :, s * width : (s + 1) * width
            ].astype(BF16)
        events(2 * c + 2)

    for d in range(n):
        block_copy(d).wait()
    acc[...] = jnp.zeros_like(acc)
    unit = 2 * chunks
    for c in range(chunks - 1):
        for low, high in ((0, half), (half, n)):
            project(c, low, high, 0, True)
            project(c, low, high, 1, False)
            unit += 1
            events(unit)
    last = chunks - 1
    for later in range(unit + 1, 2 * chunks + half):
        events(later)
    project(last, 0, n, 1 - core, True)
    exchange = pltpu.make_async_remote_copy(
        src_ref=acc.at[1 - core], dst_ref=swap, send_sem=swap_send, recv_sem=swap_recv,
        device_id={"dp": 1 - core}, device_id_type=MESH,
    )
    exchange.start()
    project(last, 0, n, core, False)
    exchange.wait()
    out[...] = (acc[core] + swap[...]).astype(BF16)

    for c in range(chunks):
        for place in range(half):
            pass_on(c, place, 0).wait_send()

            @pl.when(jnp.logical_and(place <= z, has_above))
            def _():
                pass_on(c, place, 1).wait_send()

            @pl.when(jnp.logical_and(place >= z, has_below))
            def _():
                pass_on(c, place, 2).wait_send()


def fold_and_project(n, member, rot_in_t, rot_out, eigen, rows_back, panel, block=512):
    tokens, seqs = member.shape
    feats, cols = eigen.shape
    rows, depth = rows_back.shape[0], panel.shape[0]
    parts = spans(cols)
    widest = max(width for _, width in parts)
    vmem = pl.BlockSpec(memory_space=pltpu.VMEM)
    hbm = pl.BlockSpec(memory_space=pl.ANY)
    return pl.pallas_call(
        functools.partial(fold_kernel, n, block),
        in_specs=[vmem, vmem, vmem, hbm, vmem, hbm],
        out_specs=vmem,
        out_shape=jax.ShapeDtypeStruct((seqs * rows, cols), BF16),
        scratch_shapes=[
            pltpu.VMEM((feats, cols), F32),
            pltpu.VMEM((n, depth, cols), BF16),
            pltpu.VMEM((tokens, seqs * widest), BF16),
            pltpu.VMEM((rows, seqs * widest), F32),
            pltpu.VMEM((2, seqs * rows, cols), F32),
            pltpu.VMEM((seqs * rows, cols), F32),
            *[pltpu.VMEM((n, seqs * rows, width), BF16) for _, width in parts],
            pltpu.SemaphoreType.DMA((len(parts),)),
            pltpu.SemaphoreType.DMA((n,)),
            pltpu.SemaphoreType.DMA((len(parts), n // 2, 3)),
            pltpu.SemaphoreType.DMA((len(parts), n)),
            pltpu.SemaphoreType.DMA,
            pltpu.SemaphoreType.DMA,
        ],
        compiler_params=pltpu.CompilerParams(
            collective_id=1, has_side_effects=True, vmem_limit_bytes=61 * 2**20
        ),
        cost_estimate=pl.CostEstimate(
            flops=2 * seqs * feats * cols * (tokens + 256),
            bytes_accessed=feats * cols * 4 + panel.size * 2,
            transcendentals=0,
        ),
    )(member, rot_in_t, rot_out, eigen, rows_back, panel)


def on_device(acts, out_grads, basis_in, basis_out, eigen, lengths):
    ranks = lax.axis_size("mp")
    cols = eigen.shape[1]
    rot_local = jnp.dot(acts, basis_in, preferred_element_type=F32).astype(BF16)
    grads_all = lax.all_gather(out_grads, "dp", axis=0, tiled=True)
    tokens, seqs = grads_all.shape[0], lengths.shape[0]
    shared = jnp.concatenate([rot_local, basis_in[:OUT_ROWS]], axis=0)
    shared = lax.all_gather(shared, "mp", axis=1, tiled=True)
    rows_back = shared[rot_local.shape[0] :]
    rot_in = lax.all_gather(shared[: rot_local.shape[0]], "dp", axis=0, tiled=True)
    seq_ends = jnp.cumsum(lengths)
    seq_starts = seq_ends - lengths
    position = jnp.arange(tokens, dtype=jnp.int32)[:, None]
    member = ((position >= seq_starts) & (position < seq_ends)).astype(BF16)

    if ranks % 2 == 0 and 4 <= ranks <= 8 and cols % 128 == 0:
        rot_out = scatter_sum(ranks, grads_all, basis_out)
        result = fold_and_project(
            ranks, member, rot_in.T, rot_out, eigen, rows_back, basis_out
        )
        return result.reshape(seqs, OUT_ROWS, cols)

    partial = lax.dot_general(
        basis_out, grads_all, (((0,), (1,)), ((), ())), preferred_element_type=F32
    )
    rot_out = lax.psum_scatter(partial, "mp", scatter_dimension=0, tiled=True).astype(BF16)
    masked = rot_out[None, :, :] * member.T[:, None, :]
    unscaled = jnp.einsum("tk,sjt->skj", rot_in, masked, preferred_element_type=F32)
    scaled = (unscaled / eigen[None, :, :]).astype(BF16)
    back_rot = jnp.einsum("ok,skj->soj", rows_back, scaled, preferred_element_type=F32)
    partial_out = jnp.einsum(
        "sok,fk->sof",
        lax.all_gather(back_rot.astype(BF16), "mp", axis=2, tiled=True),
        basis_out,
        preferred_element_type=F32,
    )
    return lax.psum_scatter(partial_out, "dp", scatter_dimension=2, tiled=True).astype(BF16)


def solution(mesh):
    placed = (
        P(("groups", "dp"), None),
        P(("groups", "dp"), "mp"),
        P(None, "mp"),
        P("mp", "dp"),
        P(None, ("dp", "mp")),
        P("groups"),
    )
    return jax.shard_map(
        on_device,
        mesh=mesh,
        in_specs=placed,
        out_specs=P("groups", None, ("mp", "dp")),
        check_vma=False,
    )
```

```python
import functools

import jax
import jax.numpy as jnp
from jax import lax
from jax.experimental import pallas as pl
from jax.experimental.pallas import tpu as pltpu
from jax.sharding import PartitionSpec as P

OUT_ROWS = 32
BF16 = jnp.bfloat16
F32 = jnp.float32
MESH = pl.DeviceIdType.MESH


def scatter_kernel(
    n, grads_own, feat_t, rows, panel, out, shared, grads, blocks, own, ysend, yrecv,
    zsend, zrecv, block_sem, ys_sem, yr_sem, zs_sem, zr_sem, fs_sem, fr_sem, fc_sem,
    grads_sem,
):
    cols = out.shape[1]
    feats, tokens = feat_t.shape
    half = n // 2
    me, core = lax.axis_index("mp"), lax.axis_index("dp")
    y, z = lax.rem(me, 2), lax.div(me, 2)
    partner, above, below = me + 1 - 2 * y, me + 2, me - 2
    has_above, has_below = z < half - 1, z > 0

    def row(i):
        rising = jnp.where(i < half - 1 - z, half - 1 - i, i - (half - 1 - z))
        falling = jnp.where(i < z, i, half - 1 - (i - z))
        return jnp.where(2 * z < half, rising, falling)

    def block_copy(i, j):
        lane = jnp.where(j == 0, 1 - y, y)
        start = pl.multiple_of((row(i) * 2 + lane) * cols, 128)
        return pltpu.make_async_copy(
            panel.at[:, pl.ds(start, cols)], blocks.at[2 * i + j], block_sem.at[2 * i + j]
        )

    def y_copy(i):
        return pltpu.make_async_remote_copy(
            src_ref=ysend.at[i], dst_ref=yrecv.at[i], send_sem=ys_sem.at[i],
            recv_sem=yr_sem.at[i], device_id={"mp": partner}, device_id_type=MESH,
        )

    def z_copy(i, way, target):
        slot = row(i)
        return pltpu.make_async_remote_copy(
            src_ref=zsend.at[i], dst_ref=zrecv.at[way, slot], send_sem=zs_sem.at[i],
            recv_sem=zr_sem.at[way, slot], device_id={"mp": target}, device_id_type=MESH,
        )

    lanes = pl.ds(pl.multiple_of(core * tokens, 128), tokens)
    their_lanes = pl.ds(pl.multiple_of((1 - core) * tokens, 128), tokens)
    own_rows = pl.ds(pl.multiple_of(core * tokens, 16), tokens)

    def item_copy(slot, kind):
        block = shared.at[slot, :, lanes]
        if kind == 3:
            return pltpu.make_async_remote_copy(
                src_ref=block, dst_ref=block, send_sem=fs_sem.at[slot, 3],
                recv_sem=fc_sem.at[slot], device_id={"dp": 1 - core}, device_id_type=MESH,
            )
        return pltpu.make_async_remote_copy(
            src_ref=block, dst_ref=block, send_sem=fs_sem.at[slot, kind],
            recv_sem=fr_sem.at[slot], device_id={"mp": (partner, above, below)[kind]},
            device_id_type=MESH,
        )

    def onward(slot, up, down):
        if up:

            @pl.when(has_above)
            def _():
                item_copy(slot, 1).start()

        if down:

            @pl.when(has_below)
            def _():
                item_copy(slot, 2).start()

        item_copy(slot, 3).start()

    def item_hop(h):
        for lane in range(2):

            @pl.when(z - h >= 0)
            def _():
                slot = (z - h) * 2 + lane
                item_copy(slot, 0).wait_recv()
                onward(slot, True, False)

            @pl.when(z + h <= half - 1)
            def _():
                slot = (z + h) * 2 + lane
                item_copy(slot, 0).wait_recv()
                onward(slot, False, True)

    for i in range(half):
        for j in range(2):
            block_copy(i, j).start()
    shared[me, :feats, lanes] = feat_t[...]
    share = rows.shape[0] // 2
    for q in range(feats // 128):
        shared[me, feats + q * share : feats + (q + 1) * share, lanes] = rows[
            pl.ds(pl.multiple_of(core * share, 16), share), q * 128 : (q + 1) * 128
        ]
    grads[own_rows, :] = grads_own[...]
    greet(partner, above, below, has_above, has_below, 1 - core)
    grads_copy = pltpu.make_async_remote_copy(
        src_ref=grads.at[own_rows], dst_ref=grads.at[own_rows],
        send_sem=grads_sem.at[0], recv_sem=grads_sem.at[1],
        device_id={"dp": 1 - core}, device_id_type=MESH,
    )
    grads_copy.start()
    item_copy(me, 0).start()
    onward(me, True, True)
    grads_copy.wait_recv()

    def products(i):
        block_copy(i, 0).wait()
        ysend[i] = jnp.dot(
            grads[...], blocks[2 * i], preferred_element_type=F32
        ).astype(BF16)
        y_copy(i).start()
        block_copy(i, 1).wait()
        own[i] = jnp.dot(grads[...], blocks[2 * i + 1], preferred_element_type=F32)

    for i in range(half):
        products(i)
        if i == 0:
            item_copy(partner, 0).wait_recv()
            onward(partner, True, True)
        else:
            item_hop(i)

    for i in range(half):
        y_copy(i).wait_recv()
        own[i] += yrecv[i].astype(F32)
        slot = row(i)
        upward, downward = slot > z, slot < z
        if i == half - 1:
            upward = downward = True

        @pl.when(jnp.logical_and(upward, has_below))
        def _():
            z_copy(i, 0, above).wait_recv()
            own[i] += zrecv[0, slot].astype(F32)

        @pl.when(jnp.logical_and(downward, has_above))
        def _():
            z_copy(i, 1, below).wait_recv()
            own[i] += zrecv[1, slot].astype(F32)

        if i < half - 1:
            zsend[i] = own[i].astype(BF16)

            @pl.when(upward)
            def _():
                z_copy(i, 0, above).start()

            @pl.when(downward)
            def _():
                z_copy(i, 1, below).start()
        else:
            out[...] = own[i].astype(BF16)

    for i in range(half):
        y_copy(i).wait_send()
        if i < half - 1:
            z_copy(i, 0, above).wait_send()

    grads_copy.wait_send()
    item_copy(me, 0).wait_send()
    for slot in range(n):
        item_copy(slot, 3).wait_send()

        @pl.when(jnp.logical_and(slot // 2 <= z, has_above))
        def _():
            item_copy(slot, 1).wait_send()

        @pl.when(jnp.logical_and(slot // 2 >= z, has_below))
        def _():
            item_copy(slot, 2).wait_send()

        pltpu.make_async_remote_copy(
            src_ref=shared.at[slot, :, their_lanes], dst_ref=shared.at[slot, :, their_lanes],
            send_sem=fs_sem.at[slot, 3], recv_sem=fc_sem.at[slot],
            device_id={"dp": 1 - core}, device_id_type=MESH,
        ).wait_recv()


def greet(partner, above, below, has_above, has_below, core=None):
    barrier = pltpu.get_barrier_semaphore()
    pl.semaphore_signal(barrier, inc=1, device_id={"mp": partner}, device_id_type=MESH)
    if core is not None:
        pl.semaphore_signal(barrier, inc=1, device_id={"dp": core}, device_id_type=MESH)

    @pl.when(has_above)
    def _():
        pl.semaphore_signal(barrier, inc=1, device_id={"mp": above}, device_id_type=MESH)

    @pl.when(has_below)
    def _():
        pl.semaphore_signal(barrier, inc=1, device_id={"mp": below}, device_id_type=MESH)

    fixed = 1 if core is None else 2
    pl.semaphore_wait(
        barrier, fixed + has_above.astype(jnp.int32) + has_below.astype(jnp.int32)
    )


def scatter_sum(n, grads, feat_t, rows, panel):
    tokens, depth = 2 * grads.shape[0], grads.shape[1]
    feats = feat_t.shape[0]
    extra = rows.shape[0] // 2 * (feats // 128)
    cols = panel.shape[1] // n
    half = n // 2
    return pl.pallas_call(
        functools.partial(scatter_kernel, n),
        in_specs=[
            pl.BlockSpec(memory_space=pltpu.VMEM),
            pl.BlockSpec(memory_space=pltpu.VMEM),
            pl.BlockSpec(memory_space=pltpu.VMEM),
            pl.BlockSpec(memory_space=pl.ANY),
        ],
        out_specs=[pl.BlockSpec(memory_space=pltpu.VMEM)] * 2,
        out_shape=[
            jax.ShapeDtypeStruct((tokens, cols), BF16),
            jax.ShapeDtypeStruct((n, feats + extra, tokens), BF16),
        ],
        scratch_shapes=[
            pltpu.VMEM((tokens, depth), BF16),
            pltpu.VMEM((n, depth, cols), BF16),
            pltpu.VMEM((half, tokens, cols), F32),
            pltpu.VMEM((half, tokens, cols), BF16),
            pltpu.VMEM((half, tokens, cols), BF16),
            pltpu.VMEM((half, tokens, cols), BF16),
            pltpu.VMEM((2, half, tokens, cols), BF16),
            pltpu.SemaphoreType.DMA((n,)),
            pltpu.SemaphoreType.DMA((half,)),
            pltpu.SemaphoreType.DMA((half,)),
            pltpu.SemaphoreType.DMA((half,)),
            pltpu.SemaphoreType.DMA((2, half)),
            pltpu.SemaphoreType.DMA((n, 4)),
            pltpu.SemaphoreType.DMA((n,)),
            pltpu.SemaphoreType.DMA((n,)),
            pltpu.SemaphoreType.DMA((2,)),
        ],
        compiler_params=pltpu.CompilerParams(
            collective_id=0, has_side_effects=True, vmem_limit_bytes=48 * 2**20
        ),
        cost_estimate=pl.CostEstimate(
            flops=2 * tokens * depth * cols * n,
            bytes_accessed=panel.size * 2,
            transcendentals=0,
        ),
    )(grads, feat_t, rows, panel)


def spans(cols, width=256):
    return [(start, min(width, cols - start)) for start in range(0, cols, width)]


def fold_kernel(
    n, member, shared, rot_out, eigen, panel, out,
    eig, blocks, masked, total, acc, swap, rows_back, *rest,
):
    parts = spans(out.shape[1])
    chunks = len(parts)
    held = rest[:chunks]
    eig_sem, block_sem, send_sem, recv_sem, swap_send, swap_recv = rest[chunks:]
    feats, cols = eigen.shape
    seqs, rows = member.shape[1], rows_back.shape[0]
    half = n // 2
    block, share = feats // n, rows // 2
    me, core = lax.axis_index("mp"), lax.axis_index("dp")
    y, z = lax.rem(me, 2), lax.div(me, 2)
    partner, above, below = me + 1 - 2 * y, me + 2, me - 2
    has_above, has_below = z < half - 1, z > 0

    def eig_copy(c):
        start, width = parts[c]
        span = pl.ds(start, width)
        return pltpu.make_async_copy(eigen.at[:, span], eig.at[:, span], eig_sem.at[c])

    def block_copy(d):
        start = pl.multiple_of(d * cols, 128)
        return pltpu.make_async_copy(
            panel.at[:, pl.ds(start, cols)], blocks.at[d], block_sem.at[d]
        )

    def pass_on(c, place, kind):
        slot = place * 2 + y
        return pltpu.make_async_remote_copy(
            src_ref=held[c].at[slot], dst_ref=held[c].at[slot],
            send_sem=send_sem.at[c, place, kind], recv_sem=recv_sem.at[c, slot],
            device_id={"mp": (partner, above, below)[kind]}, device_id_type=MESH,
        )

    def arrived(c, slot):
        pltpu.make_async_remote_copy(
            src_ref=held[c].at[slot], dst_ref=held[c].at[slot],
            send_sem=send_sem.at[c, 0, 0], recv_sem=recv_sem.at[c, slot],
            device_id={"mp": partner}, device_id_type=MESH,
        ).wait_recv()

    def send_own(c):
        @pl.when(has_above)
        def _():
            pass_on(c, z, 1).start()

        @pl.when(has_below)
        def _():
            pass_on(c, z, 2).start()

        pass_on(c, z, 0).start()

    def hop(c, h):
        @pl.when(z - h >= 0)
        def _():
            arrived(c, (z - h) * 2 + y)

            @pl.when(has_above)
            def _():
                pass_on(c, z - h, 1).start()

            pass_on(c, z - h, 0).start()

        @pl.when(z + h <= half - 1)
        def _():
            arrived(c, (z + h) * 2 + y)

            @pl.when(has_below)
            def _():
                pass_on(c, z + h, 2).start()

            pass_on(c, z + h, 0).start()

    def events(unit):
        for c in range(chunks):
            h = unit - 2 * (c + 1)
            if h == 0:
                send_own(c)
            elif 0 < h < half:
                hop(c, h)

    def fold_part(c, low, high):
        start, width = parts[c]

        def body(k, carry):
            at = pl.ds(pl.multiple_of(k * block, block), block)
            inverse = 1.0 / eig[at, start : start + width]
            unscaled = jnp.dot(
                shared[k, :block, :], masked[:, : seqs * width], preferred_element_type=F32
            )
            scaled = (unscaled * jnp.concatenate([inverse] * seqs, axis=1)).astype(BF16)
            total[:, : seqs * width] += jnp.dot(
                rows_back[:, at], scaled, preferred_element_type=F32
            )
            return carry

        lax.fori_loop(low, high, body, 0)

    def project(c, low, high, part, wait):
        start, width = parts[c]
        at = pl.ds(pl.multiple_of(part * cols, 128), cols)

        def body(d, carry):
            if wait:

                @pl.when(lax.rem(d, 2) != y)
                def _():
                    arrived(c, d)

            acc[part] += lax.dot_general(
                held[c][d], blocks[d, at, start : start + width],
                (((1,), (1,)), ((), ())), preferred_element_type=F32,
            )
            return carry

        lax.fori_loop(low, high, body, 0)

    for c in range(chunks):
        eig_copy(c).start()
    for d in range(n):
        block_copy(d).start()
    for d in range(n):
        for half_row in range(2):
            for q in range(block // 128):
                at = block + q * share
                rows_back[
                    half_row * share : (half_row + 1) * share,
                    d * block + q * 128 : d * block + (q + 1) * 128,
                ] = shared[d, at : at + share, half_row * 128 : (half_row + 1) * 128]
    greet(partner, above, below, has_above, has_below, 1 - core)

    steps = feats // block
    for c, (start, width) in enumerate(parts):
        for s in range(seqs):
            masked[:, s * width : (s + 1) * width] = (
                rot_out[:, start : start + width] * member[:, s : s + 1]
            )
        total[...] = jnp.zeros_like(total)
        eig_copy(c).wait()
        fold_part(c, 0, steps // 2)
        events(2 * c + 1)
        fold_part(c, steps // 2, steps)
        for s in range(seqs):
            held[c][me, s * rows : (s + 1) * rows, :] = total[
                :, s * width : (s + 1) * width
            ].astype(BF16)
        events(2 * c + 2)

    for d in range(n):
        block_copy(d).wait()
    acc[...] = jnp.zeros_like(acc)
    unit = 2 * chunks
    for c in range(chunks - 1):
        for low, high in ((0, half), (half, n)):
            project(c, low, high, 0, True)
            project(c, low, high, 1, False)
            unit += 1
            events(unit)
    last = chunks - 1
    for later in range(unit + 1, 2 * chunks + half):
        events(later)
    project(last, 0, n, 1 - core, True)
    exchange = pltpu.make_async_remote_copy(
        src_ref=acc.at[1 - core], dst_ref=swap, send_sem=swap_send, recv_sem=swap_recv,
        device_id={"dp": 1 - core}, device_id_type=MESH,
    )
    exchange.start()
    project(last, 0, n, core, False)
    exchange.wait()
    out[...] = (acc[core] + swap[...]).astype(BF16)

    for c in range(chunks):
        for place in range(half):
            pass_on(c, place, 0).wait_send()

            @pl.when(jnp.logical_and(place <= z, has_above))
            def _():
                pass_on(c, place, 1).wait_send()

            @pl.when(jnp.logical_and(place >= z, has_below))
            def _():
                pass_on(c, place, 2).wait_send()


def fold_and_project(n, member, shared, rot_out, eigen, rows, panel):
    tokens, seqs = member.shape
    feats, cols = eigen.shape
    depth = panel.shape[0]
    parts = spans(cols)
    widest = max(width for _, width in parts)
    vmem = pl.BlockSpec(memory_space=pltpu.VMEM)
    hbm = pl.BlockSpec(memory_space=pl.ANY)
    return pl.pallas_call(
        functools.partial(fold_kernel, n),
        in_specs=[vmem, vmem, vmem, hbm, hbm],
        out_specs=vmem,
        out_shape=jax.ShapeDtypeStruct((seqs * rows, cols), BF16),
        scratch_shapes=[
            pltpu.VMEM((feats, cols), F32),
            pltpu.VMEM((n, depth, cols), BF16),
            pltpu.VMEM((tokens, seqs * widest), BF16),
            pltpu.VMEM((rows, seqs * widest), F32),
            pltpu.VMEM((2, seqs * rows, cols), F32),
            pltpu.VMEM((seqs * rows, cols), F32),
            pltpu.VMEM((rows, feats), BF16),
            *[pltpu.VMEM((n, seqs * rows, width), BF16) for _, width in parts],
            pltpu.SemaphoreType.DMA((len(parts),)),
            pltpu.SemaphoreType.DMA((n,)),
            pltpu.SemaphoreType.DMA((len(parts), n // 2, 3)),
            pltpu.SemaphoreType.DMA((len(parts), n)),
            pltpu.SemaphoreType.DMA,
            pltpu.SemaphoreType.DMA,
        ],
        compiler_params=pltpu.CompilerParams(
            collective_id=1, has_side_effects=True, vmem_limit_bytes=61 * 2**20
        ),
        cost_estimate=pl.CostEstimate(
            flops=2 * seqs * feats * cols * (tokens + 256),
            bytes_accessed=feats * cols * 4 + panel.size * 2,
            transcendentals=0,
        ),
    )(member, shared, rot_out, eigen, panel)


def on_device(acts, out_grads, basis_in, basis_out, eigen, lengths):
    ranks = lax.axis_size("mp")
    cols = eigen.shape[1]
    tokens, seqs = 2 * out_grads.shape[0], lengths.shape[0]
    seq_ends = jnp.cumsum(lengths)
    seq_starts = seq_ends - lengths
    position = jnp.arange(tokens, dtype=jnp.int32)[:, None]
    member = ((position >= seq_starts) & (position < seq_ends)).astype(BF16)
    rows = basis_in[:OUT_ROWS]

    if (
        ranks in (4, 8)
        and cols % 128 == 0
        and basis_in.shape[1] % 128 == 0
        and acts.shape[0] == 128
    ):
        feat_t = lax.dot_general(
            basis_in, acts, (((0,), (1,)), ((), ())), preferred_element_type=F32
        ).astype(BF16)
        rot_out, shared = scatter_sum(ranks, out_grads, feat_t, rows, basis_out)
        result = fold_and_project(
            ranks, member, shared, rot_out, eigen, OUT_ROWS, basis_out
        )
        return result.reshape(seqs, OUT_ROWS, cols)

    rot_local = jnp.dot(acts, basis_in, preferred_element_type=F32).astype(BF16)
    grads_all = lax.all_gather(out_grads, "dp", axis=0, tiled=True)
    shared = lax.all_gather(jnp.concatenate([rot_local, rows], axis=0), "mp", axis=1, tiled=True)
    rows_back = shared[rot_local.shape[0] :]
    rot_in = lax.all_gather(shared[: rot_local.shape[0]], "dp", axis=0, tiled=True)
    partial = lax.dot_general(
        basis_out, grads_all, (((0,), (1,)), ((), ())), preferred_element_type=F32
    )
    rot_out = lax.psum_scatter(partial, "mp", scatter_dimension=0, tiled=True).astype(BF16)
    masked = rot_out[None, :, :] * member.T[:, None, :]
    unscaled = jnp.einsum("tk,sjt->skj", rot_in, masked, preferred_element_type=F32)
    scaled = (unscaled / eigen[None, :, :]).astype(BF16)
    back_rot = jnp.einsum("ok,skj->soj", rows_back, scaled, preferred_element_type=F32)
    partial_out = jnp.einsum(
        "sok,fk->sof",
        lax.all_gather(back_rot.astype(BF16), "mp", axis=2, tiled=True),
        basis_out,
        preferred_element_type=F32,
    )
    return lax.psum_scatter(partial_out, "dp", scatter_dimension=2, tiled=True).astype(BF16)


def solution(mesh):
    placed = (
        P(("groups", "dp"), None),
        P(("groups", "dp"), "mp"),
        P(None, "mp"),
        P("mp", "dp"),
        P(None, ("dp", "mp")),
        P("groups"),
    )
    return jax.shard_map(
        on_device,
        mesh=mesh,
        in_specs=placed,
        out_specs=P("groups", None, ("mp", "dp")),
        check_vma=False,
    )
```

```python
import functools

import jax
import jax.numpy as jnp
from jax import lax
from jax.experimental import pallas as pl
from jax.experimental.pallas import tpu as pltpu
from jax.sharding import PartitionSpec as P

OUT_ROWS = 32
BF16 = jnp.bfloat16
F32 = jnp.float32
MESH = pl.DeviceIdType.MESH


def scatter_kernel(
    n, grads_own, feat_t, rows, panel, out, shared, grads, blocks, own, ysend, yrecv,
    zsend, zrecv, block_sem, ys_sem, yr_sem, zs_sem, zr_sem, fs_sem, fr_sem, fc_sem,
    grads_sem,
):
    cols = out.shape[1]
    feats, tokens = feat_t.shape
    half = n // 2
    me, core = lax.axis_index("mp"), lax.axis_index("dp")
    y, z = lax.rem(me, 2), lax.div(me, 2)
    partner, above, below = me + 1 - 2 * y, me + 2, me - 2
    has_above, has_below = z < half - 1, z > 0

    def row(i):
        rising = jnp.where(i < half - 1 - z, half - 1 - i, i - (half - 1 - z))
        falling = jnp.where(i < z, i, half - 1 - (i - z))
        return jnp.where(2 * z < half, rising, falling)

    def block_copy(i, j):
        lane = 1 - y if j == 0 else y
        start = pl.multiple_of((row(i) * 2 + lane) * cols, 128)
        return pltpu.make_async_copy(
            panel.at[:, pl.ds(start, cols)], blocks.at[2 * i + j], block_sem.at[2 * i + j]
        )

    def y_copy(i):
        return pltpu.make_async_remote_copy(
            src_ref=ysend.at[i], dst_ref=yrecv.at[i], send_sem=ys_sem.at[i],
            recv_sem=yr_sem.at[i], device_id={"mp": partner}, device_id_type=MESH,
        )

    def z_copy(i, way, target):
        slot = row(i)
        return pltpu.make_async_remote_copy(
            src_ref=zsend.at[i], dst_ref=zrecv.at[way, slot], send_sem=zs_sem.at[i],
            recv_sem=zr_sem.at[way, slot], device_id={"mp": target}, device_id_type=MESH,
        )

    lanes = pl.ds(pl.multiple_of(core * tokens, 128), tokens)
    their_lanes = pl.ds(pl.multiple_of((1 - core) * tokens, 128), tokens)
    own_rows = pl.ds(pl.multiple_of(core * tokens, 16), tokens)

    def item_copy(slot, kind):
        block = shared.at[slot, :, lanes]
        if kind == 3:
            return pltpu.make_async_remote_copy(
                src_ref=block, dst_ref=block, send_sem=fs_sem.at[slot, 3],
                recv_sem=fc_sem.at[slot], device_id={"dp": 1 - core}, device_id_type=MESH,
            )
        return pltpu.make_async_remote_copy(
            src_ref=block, dst_ref=block, send_sem=fs_sem.at[slot, kind],
            recv_sem=fr_sem.at[slot], device_id={"mp": (partner, above, below)[kind]},
            device_id_type=MESH,
        )

    def onward(slot, up, down):
        if up:

            @pl.when(has_above)
            def _():
                item_copy(slot, 1).start()

        if down:

            @pl.when(has_below)
            def _():
                item_copy(slot, 2).start()

        item_copy(slot, 3).start()

    def item_hop(h):
        for lane in range(2):

            @pl.when(z - h >= 0)
            def _():
                slot = (z - h) * 2 + lane
                item_copy(slot, 0).wait_recv()
                onward(slot, True, False)

            @pl.when(z + h <= half - 1)
            def _():
                slot = (z + h) * 2 + lane
                item_copy(slot, 0).wait_recv()
                onward(slot, False, True)

    def taken(order):
        block_copy(order // 2, order % 2).wait()
        if order + 3 < n:
            block_copy((order + 3) // 2, (order + 3) % 2).start()

    block_copy(0, 0).start()
    shared[me, :feats, lanes] = feat_t[...]
    share = rows.shape[0] // 2
    for q in range(feats // 128):
        shared[me, feats + q * share : feats + (q + 1) * share, lanes] = rows[
            pl.ds(pl.multiple_of(core * share, 16), share), q * 128 : (q + 1) * 128
        ]
    grads[own_rows, :] = grads_own[...]
    greet(partner, above, below, has_above, has_below, 1 - core)
    grads_copy = pltpu.make_async_remote_copy(
        src_ref=grads.at[own_rows], dst_ref=grads.at[own_rows],
        send_sem=grads_sem.at[0], recv_sem=grads_sem.at[1],
        device_id={"dp": 1 - core}, device_id_type=MESH,
    )
    grads_copy.start()
    item_copy(me, 0).start()
    onward(me, True, True)
    block_copy(0, 1).start()
    block_copy(1, 0).start()
    grads_copy.wait_recv()

    def products(i):
        taken(2 * i)
        ysend[i] = jnp.dot(
            grads[...], blocks[2 * i], preferred_element_type=F32
        ).astype(BF16)
        y_copy(i).start()
        taken(2 * i + 1)
        own[i] = jnp.dot(grads[...], blocks[2 * i + 1], preferred_element_type=F32)

    for i in range(half):
        products(i)
        if i == 0:
            item_copy(partner, 0).wait_recv()
            onward(partner, True, True)
        else:
            item_hop(i)

    for i in range(half):
        y_copy(i).wait_recv()
        own[i] += yrecv[i].astype(F32)
        slot = row(i)
        upward, downward = slot > z, slot < z
        if i == half - 1:
            upward = downward = True

        @pl.when(jnp.logical_and(upward, has_below))
        def _():
            z_copy(i, 0, above).wait_recv()
            own[i] += zrecv[0, slot].astype(F32)

        @pl.when(jnp.logical_and(downward, has_above))
        def _():
            z_copy(i, 1, below).wait_recv()
            own[i] += zrecv[1, slot].astype(F32)

        if i < half - 1:
            zsend[i] = own[i].astype(BF16)

            @pl.when(upward)
            def _():
                z_copy(i, 0, above).start()

            @pl.when(downward)
            def _():
                z_copy(i, 1, below).start()
        else:
            out[...] = own[i].astype(BF16)

    for i in range(half):
        y_copy(i).wait_send()
        if i < half - 1:
            z_copy(i, 0, above).wait_send()

    grads_copy.wait_send()
    item_copy(me, 0).wait_send()
    for slot in range(n):
        item_copy(slot, 3).wait_send()

        @pl.when(jnp.logical_and(slot // 2 <= z, has_above))
        def _():
            item_copy(slot, 1).wait_send()

        @pl.when(jnp.logical_and(slot // 2 >= z, has_below))
        def _():
            item_copy(slot, 2).wait_send()

        pltpu.make_async_remote_copy(
            src_ref=shared.at[slot, :, their_lanes], dst_ref=shared.at[slot, :, their_lanes],
            send_sem=fs_sem.at[slot, 3], recv_sem=fc_sem.at[slot],
            device_id={"dp": 1 - core}, device_id_type=MESH,
        ).wait_recv()


def greet(partner, above, below, has_above, has_below, core=None):
    barrier = pltpu.get_barrier_semaphore()
    pl.semaphore_signal(barrier, inc=1, device_id={"mp": partner}, device_id_type=MESH)
    if core is not None:
        pl.semaphore_signal(barrier, inc=1, device_id={"dp": core}, device_id_type=MESH)

    @pl.when(has_above)
    def _():
        pl.semaphore_signal(barrier, inc=1, device_id={"mp": above}, device_id_type=MESH)

    @pl.when(has_below)
    def _():
        pl.semaphore_signal(barrier, inc=1, device_id={"mp": below}, device_id_type=MESH)

    fixed = 1 if core is None else 2
    pl.semaphore_wait(
        barrier, fixed + has_above.astype(jnp.int32) + has_below.astype(jnp.int32)
    )


def scatter_sum(n, grads, feat_t, rows, panel):
    tokens, depth = 2 * grads.shape[0], grads.shape[1]
    feats = feat_t.shape[0]
    extra = rows.shape[0] // 2 * (feats // 128)
    cols = panel.shape[1] // n
    half = n // 2
    return pl.pallas_call(
        functools.partial(scatter_kernel, n),
        in_specs=[
            pl.BlockSpec(memory_space=pltpu.VMEM),
            pl.BlockSpec(memory_space=pltpu.VMEM),
            pl.BlockSpec(memory_space=pltpu.VMEM),
            pl.BlockSpec(memory_space=pl.ANY),
        ],
        out_specs=[pl.BlockSpec(memory_space=pltpu.VMEM)] * 2,
        out_shape=[
            jax.ShapeDtypeStruct((tokens, cols), BF16),
            jax.ShapeDtypeStruct((n, feats + extra, tokens), BF16),
        ],
        scratch_shapes=[
            pltpu.VMEM((tokens, depth), BF16),
            pltpu.VMEM((n, depth, cols), BF16),
            pltpu.VMEM((half, tokens, cols), F32),
            pltpu.VMEM((half, tokens, cols), BF16),
            pltpu.VMEM((half, tokens, cols), BF16),
            pltpu.VMEM((half, tokens, cols), BF16),
            pltpu.VMEM((2, half, tokens, cols), BF16),
            pltpu.SemaphoreType.DMA((n,)),
            pltpu.SemaphoreType.DMA((half,)),
            pltpu.SemaphoreType.DMA((half,)),
            pltpu.SemaphoreType.DMA((half,)),
            pltpu.SemaphoreType.DMA((2, half)),
            pltpu.SemaphoreType.DMA((n, 4)),
            pltpu.SemaphoreType.DMA((n,)),
            pltpu.SemaphoreType.DMA((n,)),
            pltpu.SemaphoreType.DMA((2,)),
        ],
        compiler_params=pltpu.CompilerParams(
            collective_id=0, has_side_effects=True, vmem_limit_bytes=48 * 2**20
        ),
        cost_estimate=pl.CostEstimate(
            flops=2 * tokens * depth * cols * n,
            bytes_accessed=panel.size * 2,
            transcendentals=0,
        ),
    )(grads, feat_t, rows, panel)


def spans(cols, width=256):
    return [(start, min(width, cols - start)) for start in range(0, cols, width)]


def fold_kernel(
    n, member, shared, rot_out, eigen, panel, out,
    eig, masked, total, acc, swap, rows_back, *rest,
):
    parts = spans(out.shape[1])
    chunks = len(parts)
    held, blocks = rest[:chunks], rest[chunks : 2 * chunks]
    eig_sem, block_sem, send_sem, recv_sem, swap_send, swap_recv = rest[2 * chunks :]
    feats, cols = eigen.shape
    seqs, rows = member.shape[1], rows_back.shape[0]
    half = n // 2
    block, share = feats // n, rows // 2
    me, core = lax.axis_index("mp"), lax.axis_index("dp")
    y, z = lax.rem(me, 2), lax.div(me, 2)
    partner, above, below = me + 1 - 2 * y, me + 2, me - 2
    has_above, has_below = z < half - 1, z > 0

    def eig_copy(c, part):
        start, width = parts[c]
        at = (pl.ds(part * (feats // 2), feats // 2), pl.ds(start, width))
        return pltpu.make_async_copy(eigen.at[at], eig.at[at], eig_sem.at[c, part])

    def block_copy(c, d):
        start, width = parts[c]
        return pltpu.make_async_copy(
            panel.at[:, pl.ds(d * cols + start, width)],
            blocks[c].at[:, pl.ds(d * width, width)],
            block_sem.at[c, d],
        )

    def load(unit):
        if unit + 1 < chunks:
            for part in range(2):
                eig_copy(unit + 1, part).start()
        elif unit + 1 < 2 * chunks:
            for d in range(n):
                block_copy(unit + 1 - chunks, d).start()

    def held_slot(c, slot):
        width = parts[c][1]
        return held[c].at[:, pl.ds(pl.multiple_of(slot * width, 128), width)]

    def pass_on(c, place, kind):
        slot = place * 2 + y
        return pltpu.make_async_remote_copy(
            src_ref=held_slot(c, slot), dst_ref=held_slot(c, slot),
            send_sem=send_sem.at[c, place, kind], recv_sem=recv_sem.at[c, slot],
            device_id={"mp": (partner, above, below)[kind]}, device_id_type=MESH,
        )

    def arrived(c, slot):
        pltpu.make_async_remote_copy(
            src_ref=held_slot(c, slot), dst_ref=held_slot(c, slot),
            send_sem=send_sem.at[c, 0, 0], recv_sem=recv_sem.at[c, slot],
            device_id={"mp": partner}, device_id_type=MESH,
        ).wait_recv()

    def send_own(c):
        @pl.when(has_above)
        def _():
            pass_on(c, z, 1).start()

        @pl.when(has_below)
        def _():
            pass_on(c, z, 2).start()

        pass_on(c, z, 0).start()

    def hop(c, h):
        @pl.when(z - h >= 0)
        def _():
            arrived(c, (z - h) * 2 + y)

            @pl.when(has_above)
            def _():
                pass_on(c, z - h, 1).start()

            pass_on(c, z - h, 0).start()

        @pl.when(z + h <= half - 1)
        def _():
            arrived(c, (z + h) * 2 + y)

            @pl.when(has_below)
            def _():
                pass_on(c, z + h, 2).start()

            pass_on(c, z + h, 0).start()

    def events(unit):
        for c in range(chunks):
            h = unit - 2 * (c + 1)
            if h == 0:
                send_own(c)
            elif 0 < h < half:
                hop(c, h)

    def fold_part(c, low, high):
        start, width = parts[c]

        def body(k, carry):
            at = pl.ds(pl.multiple_of(k * block, block), block)
            inverse = 1.0 / eig[at, start : start + width]
            unscaled = jnp.dot(
                shared[k, :block, :], masked[:, : seqs * width], preferred_element_type=F32
            )
            scaled = (unscaled * jnp.concatenate([inverse] * seqs, axis=1)).astype(BF16)
            total[:, : seqs * width] += jnp.dot(
                rows_back[:, at], scaled, preferred_element_type=F32
            )
            return carry

        lax.fori_loop(low, high, body, 0)

    def project(c, part, first):
        if first:
            for d in range(n):
                block_copy(c, d).wait()

                @pl.when(d % 2 != y)
                def _():
                    arrived(c, d)

        at = pl.ds(pl.multiple_of(part * cols, 128), cols)
        product = lax.dot_general(
            held[c][...], blocks[c][at, :], (((1,), (1,)), ((), ())),
            preferred_element_type=F32,
        )
        acc[part] = product if c == 0 else acc[part] + product

    for part in range(2):
        eig_copy(0, part).start()
    for d in range(n):
        for half_row in range(2):
            for q in range(block // 128):
                at = block + q * share
                rows_back[
                    half_row * share : (half_row + 1) * share,
                    d * block + q * 128 : d * block + (q + 1) * 128,
                ] = shared[d, at : at + share, half_row * 128 : (half_row + 1) * 128]
    greet(partner, above, below, has_above, has_below, 1 - core)

    steps = feats // block
    for c, (start, width) in enumerate(parts):
        for s in range(seqs):
            masked[:, s * width : (s + 1) * width] = (
                rot_out[:, start : start + width] * member[:, s : s + 1]
            )
        total[...] = jnp.zeros_like(total)
        eig_copy(c, 0).wait()
        load(2 * c)
        fold_part(c, 0, steps // 2)
        events(2 * c + 1)
        eig_copy(c, 1).wait()
        load(2 * c + 1)
        fold_part(c, steps // 2, steps)
        for s in range(seqs):
            mine = pl.ds(pl.multiple_of(me * width, 128), width)
            held[c][s * rows : (s + 1) * rows, mine] = total[
                :, s * width : (s + 1) * width
            ].astype(BF16)
        events(2 * c + 2)

    unit = 2 * chunks
    for c in range(chunks - 1):
        for part in range(2):
            project(c, part, part == 0)
            unit += 1
            events(unit)
    last = chunks - 1
    for later in range(unit + 1, 2 * chunks + half):
        events(later)
    project(last, 1 - core, True)
    exchange = pltpu.make_async_remote_copy(
        src_ref=acc.at[1 - core], dst_ref=swap, send_sem=swap_send, recv_sem=swap_recv,
        device_id={"dp": 1 - core}, device_id_type=MESH,
    )
    exchange.start()
    project(last, core, False)
    exchange.wait()
    out[...] = (acc[core] + swap[...]).astype(BF16)

    for c in range(chunks):
        for place in range(half):
            pass_on(c, place, 0).wait_send()

            @pl.when(jnp.logical_and(place <= z, has_above))
            def _():
                pass_on(c, place, 1).wait_send()

            @pl.when(jnp.logical_and(place >= z, has_below))
            def _():
                pass_on(c, place, 2).wait_send()


def fold_and_project(n, member, shared, rot_out, eigen, rows, panel):
    tokens, seqs = member.shape
    feats, cols = eigen.shape
    depth = panel.shape[0]
    parts = spans(cols)
    widest = max(width for _, width in parts)
    vmem = pl.BlockSpec(memory_space=pltpu.VMEM)
    hbm = pl.BlockSpec(memory_space=pl.ANY)
    return pl.pallas_call(
        functools.partial(fold_kernel, n),
        in_specs=[vmem, vmem, vmem, hbm, hbm],
        out_specs=vmem,
        out_shape=jax.ShapeDtypeStruct((seqs * rows, cols), BF16),
        scratch_shapes=[
            pltpu.VMEM((feats, cols), F32),
            pltpu.VMEM((tokens, seqs * widest), BF16),
            pltpu.VMEM((rows, seqs * widest), F32),
            pltpu.VMEM((2, seqs * rows, cols), F32),
            pltpu.VMEM((seqs * rows, cols), F32),
            pltpu.VMEM((rows, feats), BF16),
            *[pltpu.VMEM((seqs * rows, n * width), BF16) for _, width in parts],
            *[pltpu.VMEM((depth, n * width), BF16) for _, width in parts],
            pltpu.SemaphoreType.DMA((len(parts), 2)),
            pltpu.SemaphoreType.DMA((len(parts), n)),
            pltpu.SemaphoreType.DMA((len(parts), n // 2, 3)),
            pltpu.SemaphoreType.DMA((len(parts), n)),
            pltpu.SemaphoreType.DMA,
            pltpu.SemaphoreType.DMA,
        ],
        compiler_params=pltpu.CompilerParams(
            collective_id=1, has_side_effects=True, vmem_limit_bytes=61 * 2**20
        ),
        cost_estimate=pl.CostEstimate(
            flops=2 * seqs * feats * cols * (tokens + 256),
            bytes_accessed=feats * cols * 4 + panel.size * 2,
            transcendentals=0,
        ),
    )(member, shared, rot_out, eigen, panel)


def on_device(acts, out_grads, basis_in, basis_out, eigen, lengths):
    ranks = lax.axis_size("mp")
    cols = eigen.shape[1]
    tokens, seqs = 2 * out_grads.shape[0], lengths.shape[0]
    seq_ends = jnp.cumsum(lengths)
    seq_starts = seq_ends - lengths
    position = jnp.arange(tokens, dtype=jnp.int32)[:, None]
    member = ((position >= seq_starts) & (position < seq_ends)).astype(BF16)
    rows = basis_in[:OUT_ROWS]

    if (
        ranks in (4, 8)
        and cols % 128 == 0
        and basis_in.shape[1] % 128 == 0
        and acts.shape[0] == 128
    ):
        feat_t = lax.dot_general(
            basis_in, acts, (((0,), (1,)), ((), ())), preferred_element_type=F32
        ).astype(BF16)
        rot_out, shared = scatter_sum(ranks, out_grads, feat_t, rows, basis_out)
        result = fold_and_project(
            ranks, member, shared, rot_out, eigen, OUT_ROWS, basis_out
        )
        return result.reshape(seqs, OUT_ROWS, cols)

    rot_local = jnp.dot(acts, basis_in, preferred_element_type=F32).astype(BF16)
    grads_all = lax.all_gather(out_grads, "dp", axis=0, tiled=True)
    shared = lax.all_gather(jnp.concatenate([rot_local, rows], axis=0), "mp", axis=1, tiled=True)
    rows_back = shared[rot_local.shape[0] :]
    rot_in = lax.all_gather(shared[: rot_local.shape[0]], "dp", axis=0, tiled=True)
    partial = lax.dot_general(
        basis_out, grads_all, (((0,), (1,)), ((), ())), preferred_element_type=F32
    )
    rot_out = lax.psum_scatter(partial, "mp", scatter_dimension=0, tiled=True).astype(BF16)
    masked = rot_out[None, :, :] * member.T[:, None, :]
    unscaled = jnp.einsum("tk,sjt->skj", rot_in, masked, preferred_element_type=F32)
    scaled = (unscaled / eigen[None, :, :]).astype(BF16)
    back_rot = jnp.einsum("ok,skj->soj", rows_back, scaled, preferred_element_type=F32)
    partial_out = jnp.einsum(
        "sok,fk->sof",
        lax.all_gather(back_rot.astype(BF16), "mp", axis=2, tiled=True),
        basis_out,
        preferred_element_type=F32,
    )
    return lax.psum_scatter(partial_out, "dp", scatter_dimension=2, tiled=True).astype(BF16)


def solution(mesh):
    placed = (
        P(("groups", "dp"), None),
        P(("groups", "dp"), "mp"),
        P(None, "mp"),
        P("mp", "dp"),
        P(None, ("dp", "mp")),
        P("groups"),
    )
    return jax.shard_map(
        on_device,
        mesh=mesh,
        in_specs=placed,
        out_specs=P("groups", None, ("mp", "dp")),
        check_vma=False,
    )
```

```python
import functools

import jax
import jax.numpy as jnp
from jax import lax
from jax.experimental import pallas as pl
from jax.experimental.pallas import tpu as pltpu
from jax.sharding import PartitionSpec as P

OUT_ROWS = 32
BF16 = jnp.bfloat16
F32 = jnp.float32
MESH = pl.DeviceIdType.MESH


def scatter_kernel(
    n, grads_own, feat_t, rows, panel, out, shared, grads, blocks, own, ysend, yrecv,
    zsend, zrecv, block_sem, ys_sem, yr_sem, zs_sem, zr_sem, fs_sem, fr_sem, fc_sem,
    grads_sem,
):
    cols = out.shape[1]
    feats, tokens = feat_t.shape
    half = n // 2
    me, core = lax.axis_index("mp"), lax.axis_index("dp")
    y, z = lax.rem(me, 2), lax.div(me, 2)
    partner, above, below = me + 1 - 2 * y, me + 2, me - 2
    has_above, has_below = z < half - 1, z > 0

    def row(i):
        rising = jnp.where(i < half - 1 - z, half - 1 - i, i - (half - 1 - z))
        falling = jnp.where(i < z, i, half - 1 - (i - z))
        return jnp.where(2 * z < half, rising, falling)

    def block_copy(i, j):
        lane = 1 - y if j == 0 else y
        start = pl.multiple_of((row(i) * 2 + lane) * cols, 128)
        return pltpu.make_async_copy(
            panel.at[:, pl.ds(start, cols)], blocks.at[2 * i + j], block_sem.at[2 * i + j]
        )

    def y_copy(i):
        return pltpu.make_async_remote_copy(
            src_ref=ysend.at[i], dst_ref=yrecv.at[i], send_sem=ys_sem.at[i],
            recv_sem=yr_sem.at[i], device_id={"mp": partner}, device_id_type=MESH,
        )

    def z_copy(i, way, target):
        slot = row(i)
        return pltpu.make_async_remote_copy(
            src_ref=zsend.at[i], dst_ref=zrecv.at[way, slot], send_sem=zs_sem.at[i],
            recv_sem=zr_sem.at[way, slot], device_id={"mp": target}, device_id_type=MESH,
        )

    lanes = pl.ds(pl.multiple_of(core * tokens, 128), tokens)
    their_lanes = pl.ds(pl.multiple_of((1 - core) * tokens, 128), tokens)
    own_rows = pl.ds(pl.multiple_of(core * tokens, 16), tokens)

    def item_copy(slot, kind):
        block = shared.at[slot, :, lanes]
        if kind == 3:
            return pltpu.make_async_remote_copy(
                src_ref=block, dst_ref=block, send_sem=fs_sem.at[slot, 3],
                recv_sem=fc_sem.at[slot], device_id={"dp": 1 - core}, device_id_type=MESH,
            )
        return pltpu.make_async_remote_copy(
            src_ref=block, dst_ref=block, send_sem=fs_sem.at[slot, kind],
            recv_sem=fr_sem.at[slot], device_id={"mp": (partner, above, below)[kind]},
            device_id_type=MESH,
        )

    def onward(slot, up, down):
        if up:

            @pl.when(has_above)
            def _():
                item_copy(slot, 1).start()

        if down:

            @pl.when(has_below)
            def _():
                item_copy(slot, 2).start()

        item_copy(slot, 3).start()

    def item_hop(h):
        for lane in range(2):

            @pl.when(z - h >= 0)
            def _():
                slot = (z - h) * 2 + lane
                item_copy(slot, 0).wait_recv()
                onward(slot, True, False)

            @pl.when(z + h <= half - 1)
            def _():
                slot = (z + h) * 2 + lane
                item_copy(slot, 0).wait_recv()
                onward(slot, False, True)

    def taken(order):
        block_copy(order // 2, order % 2).wait()
        if order + 3 < n:
            block_copy((order + 3) // 2, (order + 3) % 2).start()

    block_copy(0, 0).start()
    shared[me, :feats, lanes] = feat_t[...]
    share = rows.shape[0] // 2
    for q in range(feats // 128):
        shared[me, feats + q * share : feats + (q + 1) * share, lanes] = rows[
            pl.ds(pl.multiple_of(core * share, 16), share), q * 128 : (q + 1) * 128
        ]
    grads[own_rows, :] = grads_own[...]
    greet(partner, above, below, has_above, has_below, 1 - core)
    grads_copy = pltpu.make_async_remote_copy(
        src_ref=grads.at[own_rows], dst_ref=grads.at[own_rows],
        send_sem=grads_sem.at[0], recv_sem=grads_sem.at[1],
        device_id={"dp": 1 - core}, device_id_type=MESH,
    )
    grads_copy.start()
    item_copy(me, 0).start()
    onward(me, True, True)
    block_copy(0, 1).start()
    block_copy(1, 0).start()
    grads_copy.wait_recv()

    def products(i):
        taken(2 * i)
        ysend[i] = jnp.dot(
            grads[...], blocks[2 * i], preferred_element_type=F32
        ).astype(BF16)
        y_copy(i).start()
        taken(2 * i + 1)
        own[i] = jnp.dot(grads[...], blocks[2 * i + 1], preferred_element_type=F32)

    for i in range(half):
        products(i)
        if i == 0:
            item_copy(partner, 0).wait_recv()
            onward(partner, True, True)
        else:
            item_hop(i)

    for i in range(half):
        y_copy(i).wait_recv()
        own[i] += yrecv[i].astype(F32)
        slot = row(i)
        upward, downward = slot > z, slot < z
        if i == half - 1:
            upward = downward = True

        @pl.when(jnp.logical_and(upward, has_below))
        def _():
            z_copy(i, 0, above).wait_recv()
            own[i] += zrecv[0, slot].astype(F32)

        @pl.when(jnp.logical_and(downward, has_above))
        def _():
            z_copy(i, 1, below).wait_recv()
            own[i] += zrecv[1, slot].astype(F32)

        if i < half - 1:
            zsend[i] = own[i].astype(BF16)

            @pl.when(upward)
            def _():
                z_copy(i, 0, above).start()

            @pl.when(downward)
            def _():
                z_copy(i, 1, below).start()
        else:
            out[...] = own[i].astype(BF16)

    for i in range(half):
        y_copy(i).wait_send()
        if i < half - 1:
            z_copy(i, 0, above).wait_send()

    grads_copy.wait_send()
    item_copy(me, 0).wait_send()
    for slot in range(n):
        item_copy(slot, 3).wait_send()

        @pl.when(jnp.logical_and(slot // 2 <= z, has_above))
        def _():
            item_copy(slot, 1).wait_send()

        @pl.when(jnp.logical_and(slot // 2 >= z, has_below))
        def _():
            item_copy(slot, 2).wait_send()

        pltpu.make_async_remote_copy(
            src_ref=shared.at[slot, :, their_lanes], dst_ref=shared.at[slot, :, their_lanes],
            send_sem=fs_sem.at[slot, 3], recv_sem=fc_sem.at[slot],
            device_id={"dp": 1 - core}, device_id_type=MESH,
        ).wait_recv()


def greet(partner, above, below, has_above, has_below, core=None):
    barrier = pltpu.get_barrier_semaphore()
    pl.semaphore_signal(barrier, inc=1, device_id={"mp": partner}, device_id_type=MESH)
    if core is not None:
        pl.semaphore_signal(barrier, inc=1, device_id={"dp": core}, device_id_type=MESH)

    @pl.when(has_above)
    def _():
        pl.semaphore_signal(barrier, inc=1, device_id={"mp": above}, device_id_type=MESH)

    @pl.when(has_below)
    def _():
        pl.semaphore_signal(barrier, inc=1, device_id={"mp": below}, device_id_type=MESH)

    fixed = 1 if core is None else 2
    pl.semaphore_wait(
        barrier, fixed + has_above.astype(jnp.int32) + has_below.astype(jnp.int32)
    )


def scatter_sum(n, grads, feat_t, rows, panel):
    tokens, depth = 2 * grads.shape[0], grads.shape[1]
    feats = feat_t.shape[0]
    extra = rows.shape[0] // 2 * (feats // 128)
    cols = panel.shape[1] // n
    half = n // 2
    return pl.pallas_call(
        functools.partial(scatter_kernel, n),
        in_specs=[
            pl.BlockSpec(memory_space=pltpu.VMEM),
            pl.BlockSpec(memory_space=pltpu.VMEM),
            pl.BlockSpec(memory_space=pltpu.VMEM),
            pl.BlockSpec(memory_space=pl.ANY),
        ],
        out_specs=[pl.BlockSpec(memory_space=pltpu.VMEM)] * 2,
        out_shape=[
            jax.ShapeDtypeStruct((tokens, cols), BF16),
            jax.ShapeDtypeStruct((n, feats + extra, tokens), BF16),
        ],
        scratch_shapes=[
            pltpu.VMEM((tokens, depth), BF16),
            pltpu.VMEM((n, depth, cols), BF16),
            pltpu.VMEM((half, tokens, cols), F32),
            pltpu.VMEM((half, tokens, cols), BF16),
            pltpu.VMEM((half, tokens, cols), BF16),
            pltpu.VMEM((half, tokens, cols), BF16),
            pltpu.VMEM((2, half, tokens, cols), BF16),
            pltpu.SemaphoreType.DMA((n,)),
            pltpu.SemaphoreType.DMA((half,)),
            pltpu.SemaphoreType.DMA((half,)),
            pltpu.SemaphoreType.DMA((half,)),
            pltpu.SemaphoreType.DMA((2, half)),
            pltpu.SemaphoreType.DMA((n, 4)),
            pltpu.SemaphoreType.DMA((n,)),
            pltpu.SemaphoreType.DMA((n,)),
            pltpu.SemaphoreType.DMA((2,)),
        ],
        compiler_params=pltpu.CompilerParams(
            collective_id=0, has_side_effects=True, vmem_limit_bytes=48 * 2**20
        ),
        cost_estimate=pl.CostEstimate(
            flops=2 * tokens * depth * cols * n,
            bytes_accessed=panel.size * 2,
            transcendentals=0,
        ),
    )(grads, feat_t, rows, panel)


def spans(cols):
    parts, start = [(0, 128)], 128
    while start < cols:
        width = 256 if cols - start > 256 else 128
        parts.append((start, width))
        start += width
    return parts


def fold_kernel(
    n, member, shared, rot_out, eigen, panel, out,
    eig, masked, total, acc, swap, rows_back, *rest,
):
    parts = spans(out.shape[1])
    chunks = len(parts)
    held, blocks = rest[:chunks], rest[chunks : 2 * chunks]
    eig_sem, block_sem, send_sem, recv_sem, swap_send, swap_recv = rest[2 * chunks :]
    feats, cols = eigen.shape
    seqs, rows = member.shape[1], rows_back.shape[0]
    half = n // 2
    block, share = feats // n, rows // 2
    me, core = lax.axis_index("mp"), lax.axis_index("dp")
    y, z = lax.rem(me, 2), lax.div(me, 2)
    partner, above, below = me + 1 - 2 * y, me + 2, me - 2
    has_above, has_below = z < half - 1, z > 0

    def eig_copy(c, part):
        start, width = parts[c]
        at = (pl.ds(part * (feats // 2), feats // 2), pl.ds(start, width))
        return pltpu.make_async_copy(eigen.at[at], eig.at[at], eig_sem.at[c, part])

    def block_copy(c, d):
        start, width = parts[c]
        return pltpu.make_async_copy(
            panel.at[:, pl.ds(d * cols + start, width)],
            blocks[c].at[:, pl.ds(d * width, width)],
            block_sem.at[c, d],
        )

    def load(unit):
        if unit + 1 < chunks:
            for part in range(2):
                eig_copy(unit + 1, part).start()
        elif unit + 1 < 2 * chunks:
            for d in range(n):
                block_copy(unit + 1 - chunks, d).start()

    def held_slot(c, slot):
        width = parts[c][1]
        return held[c].at[:, pl.ds(pl.multiple_of(slot * width, 128), width)]

    def pass_on(c, place, kind):
        slot = place * 2 + y
        return pltpu.make_async_remote_copy(
            src_ref=held_slot(c, slot), dst_ref=held_slot(c, slot),
            send_sem=send_sem.at[c, place, kind], recv_sem=recv_sem.at[c, slot],
            device_id={"mp": (partner, above, below)[kind]}, device_id_type=MESH,
        )

    def arrived(c, slot):
        pltpu.make_async_remote_copy(
            src_ref=held_slot(c, slot), dst_ref=held_slot(c, slot),
            send_sem=send_sem.at[c, 0, 0], recv_sem=recv_sem.at[c, slot],
            device_id={"mp": partner}, device_id_type=MESH,
        ).wait_recv()

    def send_own(c):
        @pl.when(has_above)
        def _():
            pass_on(c, z, 1).start()

        @pl.when(has_below)
        def _():
            pass_on(c, z, 2).start()

        pass_on(c, z, 0).start()

    def hop(c, h):
        @pl.when(z - h >= 0)
        def _():
            arrived(c, (z - h) * 2 + y)

            @pl.when(has_above)
            def _():
                pass_on(c, z - h, 1).start()

            pass_on(c, z - h, 0).start()

        @pl.when(z + h <= half - 1)
        def _():
            arrived(c, (z + h) * 2 + y)

            @pl.when(has_below)
            def _():
                pass_on(c, z + h, 2).start()

            pass_on(c, z + h, 0).start()

    def events(unit):
        for c in range(chunks):
            h = unit - 2 * (c + 1)
            if h == 0:
                send_own(c)
            elif 0 < h < half:
                hop(c, h)

    def fold_part(c, low, high):
        start, width = parts[c]

        def body(k, carry):
            at = pl.ds(pl.multiple_of(k * block, block), block)
            inverse = 1.0 / eig[at, start : start + width]
            unscaled = jnp.dot(
                shared[k, :block, :], masked[:, : seqs * width], preferred_element_type=F32
            )
            scaled = (unscaled * jnp.concatenate([inverse] * seqs, axis=1)).astype(BF16)
            total[:, : seqs * width] += jnp.dot(
                rows_back[:, at], scaled, preferred_element_type=F32
            )
            return carry

        lax.fori_loop(low, high, body, 0)

    def project(c, part, first):
        if first:
            for d in range(n):
                block_copy(c, d).wait()

                @pl.when(d % 2 != y)
                def _():
                    arrived(c, d)

        at = pl.ds(pl.multiple_of(part * cols, 128), cols)
        product = lax.dot_general(
            held[c][...], blocks[c][at, :], (((1,), (1,)), ((), ())),
            preferred_element_type=F32,
        )
        acc[part] = product if c == 0 else acc[part] + product

    for part in range(2):
        eig_copy(0, part).start()
    for d in range(n):
        for half_row in range(2):
            for q in range(block // 128):
                at = block + q * share
                rows_back[
                    half_row * share : (half_row + 1) * share,
                    d * block + q * 128 : d * block + (q + 1) * 128,
                ] = shared[d, at : at + share, half_row * 128 : (half_row + 1) * 128]
    greet(partner, above, below, has_above, has_below, 1 - core)

    steps = feats // block
    for c, (start, width) in enumerate(parts):
        for s in range(seqs):
            masked[:, s * width : (s + 1) * width] = (
                rot_out[:, start : start + width] * member[:, s : s + 1]
            )
        total[...] = jnp.zeros_like(total)
        eig_copy(c, 0).wait()
        load(2 * c)
        fold_part(c, 0, steps // 2)
        events(2 * c + 1)
        eig_copy(c, 1).wait()
        load(2 * c + 1)
        fold_part(c, steps // 2, steps)
        for s in range(seqs):
            mine = pl.ds(pl.multiple_of(me * width, 128), width)
            held[c][s * rows : (s + 1) * rows, mine] = total[
                :, s * width : (s + 1) * width
            ].astype(BF16)
        events(2 * c + 2)

    unit = 2 * chunks
    for c in range(chunks - 1):
        for part in range(2):
            project(c, part, part == 0)
            unit += 1
            events(unit)
    last = chunks - 1
    for later in range(unit + 1, 2 * chunks + half):
        events(later)
    project(last, 1 - core, True)
    exchange = pltpu.make_async_remote_copy(
        src_ref=acc.at[1 - core], dst_ref=swap, send_sem=swap_send, recv_sem=swap_recv,
        device_id={"dp": 1 - core}, device_id_type=MESH,
    )
    exchange.start()
    project(last, core, False)
    exchange.wait()
    out[...] = (acc[core] + swap[...]).astype(BF16)

    for c in range(chunks):
        for place in range(half):
            pass_on(c, place, 0).wait_send()

            @pl.when(jnp.logical_and(place <= z, has_above))
            def _():
                pass_on(c, place, 1).wait_send()

            @pl.when(jnp.logical_and(place >= z, has_below))
            def _():
                pass_on(c, place, 2).wait_send()


def fold_and_project(n, member, shared, rot_out, eigen, rows, panel):
    tokens, seqs = member.shape
    feats, cols = eigen.shape
    depth = panel.shape[0]
    parts = spans(cols)
    widest = max(width for _, width in parts)
    vmem = pl.BlockSpec(memory_space=pltpu.VMEM)
    hbm = pl.BlockSpec(memory_space=pl.ANY)
    return pl.pallas_call(
        functools.partial(fold_kernel, n),
        in_specs=[vmem, vmem, vmem, hbm, hbm],
        out_specs=vmem,
        out_shape=jax.ShapeDtypeStruct((seqs * rows, cols), BF16),
        scratch_shapes=[
            pltpu.VMEM((feats, cols), F32),
            pltpu.VMEM((tokens, seqs * widest), BF16),
            pltpu.VMEM((rows, seqs * widest), F32),
            pltpu.VMEM((2, seqs * rows, cols), F32),
            pltpu.VMEM((seqs * rows, cols), F32),
            pltpu.VMEM((rows, feats), BF16),
            *[pltpu.VMEM((seqs * rows, n * width), BF16) for _, width in parts],
            *[pltpu.VMEM((depth, n * width), BF16) for _, width in parts],
            pltpu.SemaphoreType.DMA((len(parts), 2)),
            pltpu.SemaphoreType.DMA((len(parts), n)),
            pltpu.SemaphoreType.DMA((len(parts), n // 2, 3)),
            pltpu.SemaphoreType.DMA((len(parts), n)),
            pltpu.SemaphoreType.DMA,
            pltpu.SemaphoreType.DMA,
        ],
        compiler_params=pltpu.CompilerParams(
            collective_id=1, has_side_effects=True, vmem_limit_bytes=61 * 2**20
        ),
        cost_estimate=pl.CostEstimate(
            flops=2 * seqs * feats * cols * (tokens + 256),
            bytes_accessed=feats * cols * 4 + panel.size * 2,
            transcendentals=0,
        ),
    )(member, shared, rot_out, eigen, panel)


def on_device(acts, out_grads, basis_in, basis_out, eigen, lengths):
    ranks = lax.axis_size("mp")
    cols = eigen.shape[1]
    tokens, seqs = 2 * out_grads.shape[0], lengths.shape[0]
    seq_ends = jnp.cumsum(lengths)
    seq_starts = seq_ends - lengths
    position = jnp.arange(tokens, dtype=jnp.int32)[:, None]
    member = ((position >= seq_starts) & (position < seq_ends)).astype(BF16)
    rows = basis_in[:OUT_ROWS]

    if (
        ranks in (4, 8)
        and cols % 128 == 0
        and basis_in.shape[1] % 128 == 0
        and acts.shape[0] == 128
    ):
        feat_t = lax.dot_general(
            basis_in, acts, (((0,), (1,)), ((), ())), preferred_element_type=F32
        ).astype(BF16)
        rot_out, shared = scatter_sum(ranks, out_grads, feat_t, rows, basis_out)
        result = fold_and_project(
            ranks, member, shared, rot_out, eigen, OUT_ROWS, basis_out
        )
        return result.reshape(seqs, OUT_ROWS, cols)

    rot_local = jnp.dot(acts, basis_in, preferred_element_type=F32).astype(BF16)
    grads_all = lax.all_gather(out_grads, "dp", axis=0, tiled=True)
    shared = lax.all_gather(jnp.concatenate([rot_local, rows], axis=0), "mp", axis=1, tiled=True)
    rows_back = shared[rot_local.shape[0] :]
    rot_in = lax.all_gather(shared[: rot_local.shape[0]], "dp", axis=0, tiled=True)
    partial = lax.dot_general(
        basis_out, grads_all, (((0,), (1,)), ((), ())), preferred_element_type=F32
    )
    rot_out = lax.psum_scatter(partial, "mp", scatter_dimension=0, tiled=True).astype(BF16)
    masked = rot_out[None, :, :] * member.T[:, None, :]
    unscaled = jnp.einsum("tk,sjt->skj", rot_in, masked, preferred_element_type=F32)
    scaled = (unscaled / eigen[None, :, :]).astype(BF16)
    back_rot = jnp.einsum("ok,skj->soj", rows_back, scaled, preferred_element_type=F32)
    partial_out = jnp.einsum(
        "sok,fk->sof",
        lax.all_gather(back_rot.astype(BF16), "mp", axis=2, tiled=True),
        basis_out,
        preferred_element_type=F32,
    )
    return lax.psum_scatter(partial_out, "dp", scatter_dimension=2, tiled=True).astype(BF16)


def solution(mesh):
    placed = (
        P(("groups", "dp"), None),
        P(("groups", "dp"), "mp"),
        P(None, "mp"),
        P("mp", "dp"),
        P(None, ("dp", "mp")),
        P("groups"),
    )
    return jax.shard_map(
        on_device,
        mesh=mesh,
        in_specs=placed,
        out_specs=P("groups", None, ("mp", "dp")),
        check_vma=False,
    )
```
